32 devices in a mesh: dp: 4 (over y, x), expert: 8 (over z, core).
Axes of the slice: x: 2, y: 2, z: 4, core: 2. Of those that a mesh axis runs over, the one named last changes fastest.
Arguments:
- tokens: bfloat16 [8192, 1536], P(('dp', 'expert')), may hold values from -6 to 6
- cotangent: bfloat16 [8192, 1536], P(('dp', 'expert')), may hold values from -0.59765625 to 0.59765625
- chosen: int32 [128, 8, 16], P(('dp', 'expert')), may hold values from 0 to 63, as said below
- w_router: bfloat16 [1536, 8], replicated, may hold values from -0.15625 to 0.15625
- w_gate: bfloat16 [8, 1536, 1024], P('expert', 'dp'), may hold values from -0.15625 to 0.15625
- w_up: bfloat16 [8, 1536, 1024], P('expert', 'dp'), may hold values from -0.15625 to 0.15625
- w_down: bfloat16 [8, 1024, 1536], P('expert', 'dp'), may hold values from -0.1875 to 0.1875
Outputs:
- mixed: bfloat16 [8192, 1536], P(('dp', 'expert'))
- grad_tokens: bfloat16 [8192, 1536], P(('dp', 'expert'))
- grad_gate: float32 [8, 1536, 1024], P('expert', 'dp')
- grad_up: float32 [8, 1536, 1024], P('expert', 'dp')
- down_weight_gradient: float32 [8, 1024, 1536], P('expert', 'dp')
- grad_router: float32 [1536, 8], replicated
The draws below stay inside these ranges and needn't reach their ends.
Inputs may be any that keep to these rules, and one draw needn't show every extreme that they name: `chosen`: for each aligned block of 64 token rows and each expert, 16 different row numbers within the block; so every device has exactly 64 slots for each expert.
All inputs are finite; a program needn't handle non-finite values.
Results may differ from the reference program's by a relative error of at most 0.017.
Values may be sent and summed in bfloat16 or wider, within the bound.
No kernel may reach another device: no remote copies, remote signals or barrier semaphores. Data moves between devices by JAX's collectives and lax.ppermute only.
A program may use at most 128 MiB of HBM per device.

```python
import jax
import jax.numpy as jnp
from jax import lax

D = 1536
H = 1024
BLOCK = 64
EXPERTS = 8
PICK = 16
TOKENS = 8192
NBLK = 128


def draw_chosen(key, part):
    scores = jax.random.randint(key, (NBLK, EXPERTS, BLOCK), 0, 1048576, dtype=jnp.int32)
    ranked = scores * BLOCK + lax.broadcasted_iota(jnp.int32, (NBLK, EXPERTS, BLOCK), 2)
    _, indices = lax.top_k(ranked, PICK)
    return indices.astype(jnp.int32)


def raised(array, stream_key, source, target, parts, factor):
    owner, partner = [(jnp.arange(array.shape[position]) // (array.shape[position] // parts)).reshape([-1 if axis == position else 1 for axis in range(array.ndim)]) for position in (source, target)]
    chosen = jax.random.permutation(stream_key, parts)[partner]
    strong = (owner == chosen) | (owner == (partner + parts // 2) % parts)
    return jnp.where(strong, factor * array, array)


def block_scale(stream_key, extent, cuts, smallest, largest):
    factor_of, own = 1.0, jax.random.fold_in(stream_key, 6)
    for dim, blocks in cuts:
        draws = jnp.exp(jax.random.uniform(jax.random.fold_in(own, dim), (blocks,), jnp.float32, smallest / len(cuts), largest / len(cuts)))
        factor_of = factor_of * jnp.repeat(draws, extent[dim] // blocks).reshape([-1 if axis == dim else 1 for axis in range(len(extent))])
    return factor_of


def gaussian(rng, shape, deviation, limit, cuts=(), held_as=jnp.bfloat16):
    result = deviation * jax.random.normal(rng, shape, jnp.float32)
    if cuts:
        result = result * block_scale(rng, shape, cuts, -0.22, 0.18)
    return jnp.clip(result, -limit, limit).astype(held_as)


def heavy_noise(stream_key, extent, deviation, limit, shards, heavy, held_as=jnp.bfloat16):
    result = deviation * jax.random.normal(stream_key, extent, jnp.float32)
    if shards:
        result = result * block_scale(stream_key, extent, shards, -0.22, 0.18)
    return jnp.clip(raised(result, jax.random.fold_in(stream_key, 3), *heavy), -limit, limit).astype(held_as)


def setup_inputs(seed: int = 0) -> dict:
    arg_keys = jax.random.split(jax.random.key(seed), 8)
    tokens = heavy_noise(arg_keys[0], (TOKENS, D), 1.0, 6.0, ((0, 32),), (0, 1, 32, 2.75))
    cotangent = gaussian(arg_keys[1], (TOKENS, D), 0.1, 0.59765625, ((0, 32),))
    chosen = draw_chosen(jax.random.fold_in(arg_keys[7], 71), 0)
    w_router = gaussian(arg_keys[3], (D, EXPERTS), D ** -0.5, 0.15625)
    w_gate = gaussian(arg_keys[4], (EXPERTS, D, H), D ** -0.5, 0.15625, ((0, 8), (1, 4)))
    w_up = gaussian(arg_keys[5], (EXPERTS, D, H), D ** -0.5, 0.15625, ((0, 8), (1, 4)))
    w_down = gaussian(arg_keys[6], (EXPERTS, H, D), H ** -0.5, 0.1875, ((0, 8), (1, 4)))
    return {"tokens": tokens, "cotangent": cotangent, "chosen": chosen, "w_router": w_router, "w_gate": w_gate, "w_up": w_up, "w_down": w_down}


def reference(tokens, cotangent, chosen, w_router, w_gate, w_up, w_down):
    logits = jnp.dot(tokens, w_router, preferred_element_type=jnp.float32)
    gate_values = jax.nn.sigmoid(logits)
    offsets = (jnp.arange(NBLK, dtype=jnp.int32) * BLOCK)[:, None]

    def per_expert(carried, inputs):
        combined_total, gradient_total = carried
        pick_rows, gate_column, gate_w, up_w, down_w = inputs
        slot_rows = (pick_rows + offsets).reshape(-1).astype(jnp.int32)
        chosen_rows = tokens[slot_rows]
        slot_gate_values = gate_column[slot_rows]
        pre_gate = jnp.dot(chosen_rows, gate_w, preferred_element_type=jnp.float32)
        pre_up = jnp.dot(chosen_rows, up_w, preferred_element_type=jnp.float32)
        silu_gate = jax.nn.silu(pre_gate)
        hidden = (silu_gate * pre_up).astype(jnp.bfloat16)
        expert_out = jnp.dot(hidden, down_w, preferred_element_type=jnp.float32).astype(jnp.bfloat16)
        combined_total = combined_total.at[slot_rows].add(slot_gate_values[:, None] * expert_out.astype(jnp.float32))
        cot_rows = cotangent[slot_rows]
        scaled_cot = (slot_gate_values[:, None] * cot_rows.astype(jnp.float32)).astype(jnp.bfloat16)
        slot_dots = jnp.sum(cot_rows.astype(jnp.float32) * expert_out.astype(jnp.float32), axis=1)
        dgate_column = jnp.zeros((TOKENS,), jnp.float32).at[slot_rows].set(slot_dots)
        d_hidden = jnp.dot(scaled_cot, down_w.T, preferred_element_type=jnp.float32)
        gate_sigmoid = jax.nn.sigmoid(pre_gate)
        d_pre_gate = (d_hidden * pre_up * gate_sigmoid * (1.0 + pre_gate * (1.0 - gate_sigmoid))).astype(jnp.bfloat16)
        d_pre_up = (d_hidden * silu_gate).astype(jnp.bfloat16)
        d_rows = (jnp.dot(d_pre_gate, gate_w.T, preferred_element_type=jnp.float32)
                  + jnp.dot(d_pre_up, up_w.T, preferred_element_type=jnp.float32)).astype(jnp.bfloat16)
        gradient_total = gradient_total.at[slot_rows].add(d_rows.astype(jnp.float32))
        gate_grad = jnp.dot(chosen_rows.T, d_pre_gate, preferred_element_type=jnp.float32)
        up_grad = jnp.dot(chosen_rows.T, d_pre_up, preferred_element_type=jnp.float32)
        down_grad = jnp.dot(hidden.T, scaled_cot, preferred_element_type=jnp.float32)
        return (combined_total, gradient_total), (dgate_column, gate_grad, up_grad, down_grad)

    start_sums = (jnp.zeros((TOKENS, D), jnp.float32), jnp.zeros((TOKENS, D), jnp.float32))
    inputs = (jnp.transpose(chosen, (1, 0, 2)), gate_values.T, w_gate, w_up, w_down)
    (combined_total, gradient_total), outputs = lax.scan(per_expert, start_sums, inputs)
    dgate_columns, grad_gate, grad_up, down_weight_gradient = outputs
    dgate = dgate_columns.T
    d_logit = (dgate * gate_values * (1.0 - gate_values)).astype(jnp.bfloat16)
    grad_tokens = (gradient_total + jnp.dot(d_logit, w_router.T, preferred_element_type=jnp.float32)).astype(jnp.bfloat16)
    grad_router = jnp.dot(tokens.T, d_logit, preferred_element_type=jnp.float32)
    return (combined_total.astype(jnp.bfloat16), grad_tokens, grad_gate, grad_up, down_weight_gradient, grad_router)
```

```python
import functools

import jax
import jax.numpy as jnp
from jax import lax
from jax.experimental import pallas as pl
from jax.experimental.pallas import tpu as pltpu
from jax.sharding import PartitionSpec as P

F32 = jnp.float32
BF16 = jnp.bfloat16
VMEM = pl.BlockSpec(memory_space=pltpu.VMEM)
SMEM = pl.BlockSpec(memory_space=pltpu.SMEM)


def dot(a, b, dims=((1,), (0,))):
    return lax.dot_general(a, b, (dims, ((), ())), preferred_element_type=F32)


def call(kernel, outs, args, flops, scalars=0, scratch=()):
    sizes = [a.size * a.dtype.itemsize for a in args] + [
        o.size * o.dtype.itemsize for o in outs
    ]
    return pl.pallas_call(
        kernel,
        out_shape=list(outs),
        in_specs=[SMEM] * scalars + [VMEM] * (len(args) - scalars),
        out_specs=[VMEM] * len(outs),
        scratch_shapes=list(scratch),
        compiler_params=pltpu.CompilerParams(vmem_limit_bytes=40 << 20),
        cost_estimate=pl.CostEstimate(
            flops=int(flops), bytes_accessed=int(sum(sizes)), transcendentals=0
        ),
    )(*args)


def shape(dims, dtype):
    return jax.ShapeDtypeStruct(tuple(dims), dtype)


def hop(x, axis, size, target):
    return lax.ppermute(x, axis, [(i, target(i)) for i in range(size)])


def ring_order(n):
    return [i for i in range(0, n, 2)] + [i for i in range(n - 1, 0, -2)]


def ring_hop(x, n, step):
    order = ring_order(n)
    place = {d: q for q, d in enumerate(order)}
    return hop(x, "dp", n, lambda i: order[(place[i] + step) % n])


def hits(rows_ref, start, count, tok_rows, dtype=BF16):
    line = rows_ref[:, start : start + count]
    grid = lax.broadcasted_iota(jnp.int32, (tok_rows, count), 0)
    return (grid == line).astype(F32).astype(dtype)


def pick_rows(rows_ref, src_ref, start, count):
    one = hits(rows_ref, start, count, src_ref.shape[0])
    return dot(one, src_ref[...], ((0,), (0,))).astype(BF16)


def pick_kernel(part, rows_ref, src_ref, *outs):
    for k, out in enumerate(outs):
        out[...] = pick_rows(rows_ref, src_ref, k * 2 * part, 2 * part)


def pick_split_kernel(part, chips, rows_ref, src_ref, keep_ref, give_ref):
    for k in range(chips):
        both = pick_rows(rows_ref, src_ref, k * 2 * part, 2 * part)
        keep_ref[k * part : (k + 1) * part, :] = both[:part]
        give_ref[k * part : (k + 1) * part, :] = both[part:]


def front_kernel(part, chips, n, ids, *refs):
    recs = refs[:chips]
    sw, wr = refs[chips : chips + 2]
    gates = refs[chips + 2 : chips + 2 + n]
    ups = refs[chips + 2 + n : chips + 2 + 2 * n]
    xc, hd, sa, ua, gcol, x = refs[chips + 2 + 2 * n :]
    for k in range(chips):
        x[2 * k * part : (2 * k + 1) * part, :] = recs[k][:part, :]
        x[(2 * k + 1) * part : (2 * k + 2) * part, :] = sw[k * part : (k + 1) * part, :]
    width = x.shape[1] // n
    for d in range(n):
        xc[d] = x[:, d * width : (d + 1) * width]
    logits = dot(x[...], wr[...])
    lanes = lax.broadcasted_iota(jnp.int32, logits.shape, 1)
    mine = jnp.sum(jnp.where(lanes == ids[n], logits, 0.0), axis=1, keepdims=True)
    gcol[...] = jax.nn.sigmoid(mine)
    tile = 256
    hidden = hd.shape[1]

    def step(t, carry):
        cols = pl.ds(pl.multiple_of(t * tile, tile), tile)
        a = dot(xc[ids[0]], gates[0][:, cols])
        b = dot(xc[ids[0]], ups[0][:, cols])
        for s in range(1, n):
            a = a + dot(xc[ids[s]], gates[s][:, cols])
            b = b + dot(xc[ids[s]], ups[s][:, cols])
        sig = jax.nn.sigmoid(a)
        silu = a * sig
        hd[:, cols] = (silu * b).astype(BF16)
        sa[:, cols] = silu
        ua[:, cols] = b * sig * (1.0 + a * (1.0 - sig))
        return carry

    lax.fori_loop(0, hidden // tile, step, 0)


def down_kernel(part, chips, n, ids, keep0, got0, *refs):
    recs = refs[: chips - 1]
    gcol, hd = refs[chips - 1 : chips + 1]
    c, g = refs[chips + 1 : chips + 3]
    outs = refs[chips + 3 :]
    c[:part, :] = keep0[...]
    c[part : 2 * part, :] = got0[...]
    for k in range(1, chips):
        c[2 * k * part : 2 * (k + 1) * part, :] = recs[k - 1][...]
    g[...] = (gcol[...] * c[...].astype(F32)).astype(BF16)
    width = hd.shape[1] // n
    half = n // 2

    def chunk(s):
        cols = pl.ds(pl.multiple_of(ids[s] * width, 128), width)
        return dot(hd[:, cols], g[...], ((0,), (0,))).astype(BF16)

    far = chunk(half)
    outs[0][...] = far[: width // 2]
    outs[1][...] = far[width // 2 :]
    place = 2
    for s in range(n):
        if s != half:
            outs[place][...] = chunk(s)
            place += 1


def out_kernel(part, chips, n, ids, hd, c, gcol, xc, *refs):
    downs = refs[: n + 1]
    gos = refs[n + 1 : n + 1 + chips]
    dl, router = refs[n + 1 + chips : n + 3 + chips]
    width = hd.shape[1] // n
    half = n // 2

    def term(s):
        cols = pl.ds(pl.multiple_of(ids[s] * width, 128), width)
        if s == half:
            w = jnp.concatenate([downs[half][...], downs[n][...]], axis=0)
        else:
            w = downs[s][...]
        return dot(hd[:, cols], w)

    o = term(0)
    for s in range(1, n):
        o = o + term(s)
    o = o.astype(BF16).astype(F32)
    gate = gcol[...]
    go = (gate * o).astype(BF16)
    for k in range(chips):
        gos[k][...] = go[2 * k * part : 2 * (k + 1) * part]
    dgate = jnp.sum(c[...].astype(F32) * o, axis=1, keepdims=True)
    dlogit = (dgate * gate * (1.0 - gate)).astype(BF16)
    dl[...] = dlogit.astype(F32)
    chunk = xc.shape[2]
    for d in range(n):
        router[:, d * chunk : (d + 1) * chunk] = jnp.sum(
            xc[d].astype(F32) * dlogit.astype(F32), axis=0, keepdims=True
        )


def hidden_kernel(n, ids, g, sa, ua, *refs):
    downs = refs[: n + 1]
    da, db = refs[n + 1 :]
    width = sa.shape[1] // n
    half = n // 2
    for s in range(n):
        cols = pl.ds(pl.multiple_of(ids[s] * width, 128), width)
        if s == half:
            w = jnp.concatenate([downs[half][...], downs[n][...]], axis=0)
        else:
            w = downs[s][...]
        dh = dot(g[...], w, ((1,), (1,)))
        da[:, cols] = (dh * ua[:, cols]).astype(BF16)
        db[:, cols] = (dh * sa[:, cols]).astype(BF16)


def weight_kernel(n, order, ids, xc, da, db, *outs):
    tile = 256
    for place, s in enumerate(order):
        xt = xc[ids[s]].T
        gate, up = outs[2 * place], outs[2 * place + 1]

        def step(t, carry, xt=xt, gate=gate, up=up):
            cols = pl.ds(pl.multiple_of(t * tile, tile), tile)
            gate[:, cols] = dot(xt, da[:, cols]).astype(BF16)
            up[:, cols] = dot(xt, db[:, cols]).astype(BF16)
            return carry

        lax.fori_loop(0, da.shape[1] // tile, step, 0)


def rows_kernel(part, chips, n, ids, da, db, dl, wr, *refs):
    gates = refs[:n]
    ups = refs[n : 2 * n]
    keep, give, scr = refs[2 * n :]
    for s in range(n):
        scr[ids[s]] = dot(da[...], gates[s][...], ((1,), (1,))) + dot(
            db[...], ups[s][...], ((1,), (1,))
        )
    chunk = scr.shape[2]
    for d in range(n):
        cols = slice(d * chunk, (d + 1) * chunk)
        total = (scr[d] + dl[...] * wr[:, cols].astype(F32)).astype(BF16)
        for k in range(chips):
            lo = 2 * k * part
            keep[k * part : (k + 1) * part, cols] = total[lo : lo + part]
            give[k * part : (k + 1) * part, cols] = total[lo + part : lo + 2 * part]


def mixed_kernel(part, chips, rows_ref, *refs):
    recs = refs[:chips]
    sw, out = refs[chips:]
    tok_rows = out.shape[0]
    total = None
    for k in range(chips):
        one = hits(rows_ref, 2 * k * part, 2 * part, tok_rows)
        rows = jnp.concatenate([recs[k][:part, :], sw[k * part : (k + 1) * part, :]], axis=0)
        now = dot(one, rows)
        total = now if total is None else total + now
    out[...] = total.astype(BF16)


def grad_kernel(part, chips, rows_ref, keep0, got0, *refs):
    recs = refs[: chips - 1]
    out = refs[chips - 1]
    tok_rows = out.shape[0]
    total = None
    for k in range(chips):
        one = hits(rows_ref, 2 * k * part, 2 * part, tok_rows)
        if k == 0:
            rows = jnp.concatenate([keep0[...], got0[...]], axis=0)
        else:
            rows = recs[k - 1][...]
        now = dot(one, rows)
        total = now if total is None else total + now
    out[...] = total.astype(BF16)


def body(n, experts, tokens, cotangent, chosen, w_router, w_gate, w_up, w_down):
    tok_rows, model = tokens.shape
    blocks, _, picks = chosen.shape
    block_rows = tok_rows // blocks
    part = blocks * picks
    chips = experts // 2
    slots = experts * part
    half = n // 2
    gate_w, up_w, down_w = w_gate[0], w_up[0], w_down[0]
    hidden = gate_w.shape[1]

    d_me = lax.axis_index("dp")
    e_me = lax.axis_index("expert")
    place = jnp.where(d_me % 2 == 0, d_me // 2, n - 1 - d_me // 2)
    order = jnp.asarray(ring_order(n), jnp.int32)
    ids = jnp.concatenate(
        [order[(place + jnp.arange(n, dtype=jnp.int32)) % n], e_me[None].astype(jnp.int32)]
    )

    gate_p, up_n = ring_hop(gate_w, n, 1), ring_hop(up_w, n, -1)
    up_p, gate_n = ring_hop(up_w, n, 1), ring_hop(gate_w, n, -1)

    offsets = (jnp.arange(blocks, dtype=jnp.int32) * block_rows)[:, None, None]
    peers = e_me ^ jnp.arange(experts, dtype=jnp.int32)
    rows = jnp.transpose(jnp.take(chosen + offsets, peers, axis=1), (1, 0, 2)).reshape(1, slots)

    def exchange_z(bufs):
        return [
            bufs[k] if k == 0 else hop(bufs[k], "expert", experts, lambda i, k=k: i ^ (2 * k))
            for k in range(chips)
        ]

    def swap(x):
        return hop(x, "expert", experts, lambda i: i ^ 1)

    pick_flops = 2 * slots * tok_rows * model
    x_bufs = call(
        functools.partial(pick_kernel, part),
        [shape((2 * part, model), BF16)] * chips,
        [rows, tokens],
        pick_flops,
    )
    x_recs = exchange_z(x_bufs)
    x_sw = swap(jnp.concatenate([r[part:] for r in x_recs], axis=0))

    c_keep, c_give = call(
        functools.partial(pick_split_kernel, part, chips),
        [shape((chips * part, model), BF16)] * 2,
        [rows, cotangent],
        pick_flops,
    )
    c_got = swap(c_give)
    c_recs = exchange_z(
        [
            jnp.concatenate(
                [c_keep[k * part : (k + 1) * part], c_got[k * part : (k + 1) * part]], axis=0
            )
            if k
            else None
            for k in range(chips)
        ]
    )[1:]

    gates, ups = {0: gate_w, n - 1: gate_p, 1: gate_n}, {0: up_w, n - 1: up_p, 1: up_n}
    for s in range(2, half):
        gates[n - s] = ring_hop(gates[n - s + 1], n, 1)
        ups[s] = ring_hop(ups[s - 1], n, -1)
        ups[n - s] = ring_hop(ups[n - s + 1], n, 1)
        gates[s] = ring_hop(gates[s - 1], n, -1)
    if n > 2:
        gates[half] = ring_hop(gates[half + 1], n, 1)
        ups[half] = ring_hop(ups[half - 1], n, -1)
    downs = {0: down_w}
    for s in range(1, half):
        downs[n - s] = ring_hop(downs[(n - s + 1) % n], n, 1)
        downs[s] = ring_hop(downs[s - 1], n, -1)
    cut = down_w.shape[0] // 2
    far_a = ring_hop(downs[(half + 1) % n][:cut], n, 1)
    far_b = ring_hop(downs[half - 1][cut:], n, -1)
    gate_list = [gates[s] for s in range(n)]
    up_list = [ups[s] for s in range(n)]
    down_list = [far_a if s == half else downs[s] for s in range(n)] + [far_b]

    matmul = 2 * slots * model * hidden
    xc, hd, sa, ua, gcol = call(
        functools.partial(front_kernel, part, chips, n),
        [
            shape((n, slots, model // n), BF16),
            shape((slots, hidden), BF16),
            shape((slots, hidden), F32),
            shape((slots, hidden), F32),
            shape((slots, 1), F32),
        ],
        [ids, *x_recs, x_sw, w_router, *gate_list, *up_list],
        2 * matmul,
        scalars=1,
        scratch=[pltpu.VMEM((slots, model), BF16)],
    )
    width = hidden // n
    c_all, g_all, *down_parts = call(
        functools.partial(down_kernel, part, chips, n),
        [shape((slots, model), BF16)] * 2
        + [shape((width // 2, model), BF16)] * 2
        + [shape((width, model), BF16)] * (n - 1),
        [ids, c_keep[:part], c_got[:part], *c_recs, gcol, hd],
        matmul,
        scalars=1,
    )
    *go_bufs, dl, router_row = call(
        functools.partial(out_kernel, part, chips, n),
        [shape((2 * part, model), BF16)] * chips
        + [shape((slots, 1), F32), shape((1, model), F32)],
        [ids, hd, c_all, gcol, xc, *down_list],
        matmul,
        scalars=1,
    )
    o_recs = exchange_z(go_bufs)
    o_sw = swap(jnp.concatenate([r[part:] for r in o_recs], axis=0))

    down_of = {}
    place_in = 2
    for s in range(n):
        if s != half:
            down_of[s] = down_parts[place_in]
            place_in += 1
    low = ring_hop(down_parts[0], n, 1)
    high = ring_hop(down_parts[1], n, -1)

    def plus(a, b):
        return (a.astype(F32) + b.astype(F32)).astype(BF16)

    fwd = jnp.concatenate([plus(down_of[half - 1][:cut], low), down_of[half - 1][cut:]], axis=0)
    bwd_own = down_of[(half + 1) % n]
    bwd = jnp.concatenate([bwd_own[:cut], plus(bwd_own[cut:], high)], axis=0)
    for s in range(half - 1, 0, -1):
        fwd = ring_hop(fwd, n, 1)
        bwd = ring_hop(bwd, n, -1)
        if s > 1:
            fwd, bwd = plus(down_of[s - 1], fwd), plus(down_of[n - s + 1], bwd)
    down_grad = down_of[0].astype(F32) + fwd.astype(F32) + bwd.astype(F32)

    da, db = call(
        functools.partial(hidden_kernel, n),
        [shape((slots, hidden), BF16)] * 2,
        [ids, g_all, sa, ua, *down_list],
        matmul,
        scalars=1,
    )
    order_of = [half] + [s for s in range(n) if s != half]
    grads = call(
        functools.partial(weight_kernel, n, order_of),
        [shape((model // n, hidden), BF16)] * (2 * n),
        [ids, xc, da, db],
        2 * matmul,
        scalars=1,
    )
    gate_of = {s: grads[2 * i] for i, s in enumerate(order_of)}
    up_of = {s: grads[2 * i + 1] for i, s in enumerate(order_of)}

    wr_row = lax.dynamic_slice_in_dim(w_router.T, e_me, 1, axis=0)
    r_keep, r_give = call(
        functools.partial(rows_kernel, part, chips, n),
        [shape((chips * part, model), BF16)] * 2,
        [ids, da, db, dl, wr_row, *gate_list, *up_list],
        2 * matmul,
        scalars=1,
        scratch=[pltpu.VMEM((n, slots, model // n), F32)],
    )
    r_got = swap(r_give)
    r_recs = exchange_z(
        [
            jnp.concatenate(
                [r_keep[k * part : (k + 1) * part], r_got[k * part : (k + 1) * part]], axis=0
            )
            if k
            else None
            for k in range(chips)
        ]
    )[1:]

    fwd_g, bwd_u = ring_hop(gate_of[half], n, 1), ring_hop(up_of[half], n, -1)
    fwd = (plus(gate_of[half - 1], fwd_g), up_of[half - 1])
    bwd = (gate_of[(half + 1) % n], plus(up_of[(half + 1) % n], bwd_u))
    for s in range(half - 1, 0, -1):
        fwd = tuple(ring_hop(v, n, 1) for v in fwd)
        bwd = tuple(ring_hop(v, n, -1) for v in bwd)
        if s > 1:
            fwd = (plus(gate_of[s - 1], fwd[0]), plus(up_of[s - 1], fwd[1]))
            bwd = (plus(gate_of[n - s + 1], bwd[0]), plus(up_of[n - s + 1], bwd[1]))
    grad_gate = gate_of[0].astype(F32) + fwd[0].astype(F32) + bwd[0].astype(F32)
    grad_up = up_of[0].astype(F32) + fwd[1].astype(F32) + bwd[1].astype(F32)

    total = router_row
    bit = 1
    while bit < n:
        total = total + hop(total, "dp", n, lambda i, b=bit: i ^ b)
        bit *= 2
    bit = 1
    while bit < experts:
        total = jnp.concatenate(
            [total, hop(total, "expert", experts, lambda i, b=bit: i ^ b)], axis=0
        )
        bit *= 2
    grad_router = jnp.take(total, peers, axis=0).T

    mixed = call(
        functools.partial(mixed_kernel, part, chips),
        [shape((tok_rows, model), BF16)],
        [rows, *o_recs, o_sw],
        pick_flops,
    )[0]
    grad_tokens = call(
        functools.partial(grad_kernel, part, chips),
        [shape((tok_rows, model), BF16)],
        [rows, r_keep[:part], r_got[:part], *r_recs],
        pick_flops,
    )[0]
    return (
        mixed,
        grad_tokens,
        grad_gate[None],
        grad_up[None],
        down_grad[None],
        grad_router,
    )


def solution(mesh):
    sizes = dict(mesh.shape)
    return jax.shard_map(
        functools.partial(body, sizes["dp"], sizes["expert"]),
        mesh=mesh,
        in_specs=(
            P(("dp", "expert"), None),
            P(("dp", "expert"), None),
            P(("dp", "expert"), None, None),
            P(),
            P("expert", "dp", None),
            P("expert", "dp", None),
            P("expert", "dp", None),
        ),
        out_specs=(
            P(("dp", "expert"), None),
            P(("dp", "expert"), None),
            P("expert", "dp", None),
            P("expert", "dp", None),
            P("expert", "dp", None),
            P(),
        ),
        check_vma=False,
    )
```

```python
import functools

import jax
import jax.numpy as jnp
from jax import lax
from jax.experimental import pallas as pl
from jax.experimental.pallas import tpu as pltpu
from jax.sharding import PartitionSpec as P

F32 = jnp.float32
KF, HP, HF, HS = 0, 0, 3e-05, 12e-6
BF16 = jnp.bfloat16
VMEM = pl.BlockSpec(memory_space=pltpu.VMEM)
SMEM = pl.BlockSpec(memory_space=pltpu.SMEM)


def dot(a, b, dims=((1,), (0,))):
    return lax.dot_general(a, b, (dims, ((), ())), preferred_element_type=F32)


def call(kernel, outs, args, flops, scalars=0, scratch=(), hint=0):
    sizes = [a.size * a.dtype.itemsize for a in args] + [
        o.size * o.dtype.itemsize for o in outs
    ]
    return pl.pallas_call(
        kernel,
        out_shape=list(outs),
        in_specs=[SMEM] * scalars + [VMEM] * (len(args) - scalars),
        out_specs=[VMEM] * len(outs),
        scratch_shapes=list(scratch),
        compiler_params=pltpu.CompilerParams(vmem_limit_bytes=24 << 20),
        cost_estimate=pl.CostEstimate(
            flops=int(KF * flops + hint * 1e15) + 1,
            bytes_accessed=int(KF * sum(sizes)) + 1, transcendentals=0
        ),
    )(*args)


def shape(dims, dtype):
    return jax.ShapeDtypeStruct(tuple(dims), dtype)


def after(x, *others):
    return lax.optimization_barrier((x, *others))[0]


def hop(x, axis, size, target):
    return lax.ppermute(x, axis, [(i, target(i)) for i in range(size)])


def ring_order(n):
    return [i for i in range(0, n, 2)] + [i for i in range(n - 1, 0, -2)]


def ring_hop(x, n, step):
    order = ring_order(n)
    place = {d: q for q, d in enumerate(order)}
    return hop(x, "dp", n, lambda i: order[(place[i] + step) % n])


def hits(rows_ref, start, count, tok_rows, dtype=BF16):
    line = rows_ref[:, start : start + count]
    grid = lax.broadcasted_iota(jnp.int32, (tok_rows, count), 0)
    return (grid == line).astype(F32).astype(dtype)


def pick_kernel(rows_ref, src_ref, out_ref):
    tile = 128
    for start in range(0, out_ref.shape[0], tile):
        one = hits(rows_ref, start, tile, src_ref.shape[0])
        out_ref[start : start + tile, :] = dot(one, src_ref[...], ((0,), (0,))).astype(BF16)


def front_kernel(n, ids, x, wr, *refs):
    gates = refs[:n]
    ups = refs[n : 2 * n]
    xt, hd, hdt, sa, ua, gcol, xc = refs[2 * n :]
    width = x.shape[1] // n
    for d in range(n):
        xc[d] = x[:, d * width : (d + 1) * width]
    logits = dot(x[...], wr[...])
    lanes = lax.broadcasted_iota(jnp.int32, logits.shape, 1)
    mine = jnp.sum(jnp.where(lanes == ids[n], logits, 0.0), axis=1, keepdims=True)
    gcol[...] = jax.nn.sigmoid(mine)
    tile = 256
    hidden = hd.shape[1]

    def step(t, carry):
        cols = pl.ds(pl.multiple_of(t * tile, tile), tile)
        a = dot(xc[ids[0]], gates[0][:, cols])
        b = dot(xc[ids[0]], ups[0][:, cols])
        for s in range(1, n):
            a = a + dot(xc[ids[s]], gates[s][:, cols])
            b = b + dot(xc[ids[s]], ups[s][:, cols])
        sig = jax.nn.sigmoid(a)
        silu = a * sig
        h = (silu * b).astype(BF16)
        hd[:, cols] = h
        hdt[cols, :] = h.T
        sa[:, cols] = silu
        ua[:, cols] = b * sig * (1.0 + a * (1.0 - sig))
        return carry

    lax.fori_loop(0, hidden // tile, step, 0)
    for d in range(n):
        xt[d] = xc[d].T


def chunk_of(ids, s, width):
    return pl.ds(pl.multiple_of(ids[s] * width, width), width)


def down_far_kernel(n, ids, c, gcol, hdt, g, low, high):
    g[...] = (gcol[...] * c[...].astype(F32)).astype(BF16)
    width = hdt.shape[0] // n
    far = dot(hdt[chunk_of(ids, n // 2, width), :], g[...]).astype(BF16)
    low[...] = far[: width // 2]
    high[...] = far[width // 2 :]


def down_kernel(n, ids, g, hdt, *outs):
    width = hdt.shape[0] // n
    for out, s in zip(outs, [s for s in range(n) if s != n // 2]):
        out[...] = dot(hdt[chunk_of(ids, s, width), :], g[...]).astype(BF16)


def out_kernel(n, ids, hd, gcol, *refs):
    downs = refs[: n + 1]
    go, o_ref = refs[n + 1 :]
    width = hd.shape[1] // n
    half = n // 2

    def term(s):
        cols = pl.ds(pl.multiple_of(ids[s] * width, 128), width)
        if s == half:
            w = jnp.concatenate([downs[half][...], downs[n][...]], axis=0)
        else:
            w = downs[s][...]
        return dot(hd[:, cols], w)

    o = term(0)
    for s in range(1, n):
        o = o + term(s)
    o = o.astype(BF16)
    o_ref[...] = o
    go[...] = (gcol[...] * o.astype(F32)).astype(BF16)


def hidden_kernel(n, ids, g, sa, ua, *refs):
    downs = refs[: n + 1]
    da, db = refs[n + 1 :]
    width = sa.shape[1] // n
    half = n // 2
    for s in range(n):
        cols = pl.ds(pl.multiple_of(ids[s] * width, 128), width)
        if s == half:
            w = jnp.concatenate([downs[half][...], downs[n][...]], axis=0)
        else:
            w = downs[s][...]
        dh = dot(g[...], w, ((1,), (1,)))
        da[:, cols] = (dh * ua[:, cols]).astype(BF16)
        db[:, cols] = (dh * sa[:, cols]).astype(BF16)


def router_kernel(c, o, gcol, x, dl, router):
    gate = gcol[...]
    dgate = jnp.sum(c[...].astype(F32) * o[...].astype(F32), axis=1, keepdims=True)
    dlogit = (dgate * gate * (1.0 - gate)).astype(BF16)
    dl[...] = dlogit.astype(F32)
    router[...] = dot(dlogit, x[...], ((0,), (0,)))


def weight_kernel(order, ids, xt, da, db, *outs):
    tile = 256
    for place, s in enumerate(order):
        gate, up = outs[2 * place], outs[2 * place + 1]

        def step(t, carry, s=s, gate=gate, up=up):
            cols = pl.ds(pl.multiple_of(t * tile, tile), tile)
            gate[:, cols] = dot(xt[ids[s]], da[:, cols]).astype(BF16)
            up[:, cols] = dot(xt[ids[s]], db[:, cols]).astype(BF16)
            return carry

        lax.fori_loop(0, da.shape[1] // tile, step, 0)


def rows_kernel(n, ids, da, db, dl, wr, *refs):
    gates = refs[:n]
    ups = refs[n : 2 * n]
    out, scr = refs[2 * n :]
    for s in range(n):
        scr[ids[s]] = dot(da[...], gates[s][...], ((1,), (1,))) + dot(
            db[...], ups[s][...], ((1,), (1,))
        )
    chunk = scr.shape[2]
    for d in range(n):
        cols = slice(d * chunk, (d + 1) * chunk)
        out[:, cols] = (scr[d] + dl[...] * wr[:, cols].astype(F32)).astype(BF16)


def sum_far_kernel(low, high, nxt, prv, fwd, bwd):
    cut = low.shape[0]
    fwd[:cut, :] = (nxt[:cut, :].astype(F32) + low[...].astype(F32)).astype(BF16)
    fwd[cut:, :] = nxt[cut:, :]
    bwd[:cut, :] = prv[:cut, :]
    bwd[cut:, :] = (prv[cut:, :].astype(F32) + high[...].astype(F32)).astype(BF16)


def sum_pair_kernel(a, b, c, d, first, second):
    first[...] = (a[...].astype(F32) + b[...].astype(F32)).astype(BF16)
    second[...] = (c[...].astype(F32) + d[...].astype(F32)).astype(BF16)


def scatter_kernel(rows_ref, src_ref, out_ref):
    one = hits(rows_ref, 0, src_ref.shape[0], out_ref.shape[0])
    out_ref[...] = dot(one, src_ref[...]).astype(BF16)


def body(n, experts, tokens, cotangent, chosen, w_router, w_gate, w_up, w_down):
    tok_rows, model = tokens.shape
    blocks, _, picks = chosen.shape
    block_rows = tok_rows // blocks
    part = blocks * picks
    slots = experts * part
    half = n // 2
    gate_w, up_w, down_w = w_gate[0], w_up[0], w_down[0]
    hidden = gate_w.shape[1]

    d_me = lax.axis_index("dp")
    e_me = lax.axis_index("expert")
    place = jnp.where(d_me % 2 == 0, d_me // 2, n - 1 - d_me // 2)
    order = jnp.asarray(ring_order(n), jnp.int32)
    ids = jnp.concatenate(
        [order[(place + jnp.arange(n, dtype=jnp.int32)) % n], e_me[None].astype(jnp.int32)]
    )

    gate_p, up_n = ring_hop(gate_w, n, 1), ring_hop(up_w, n, -1)
    up_p, gate_n = ring_hop(up_w, n, 1), ring_hop(gate_w, n, -1)

    offsets = (jnp.arange(blocks, dtype=jnp.int32) * block_rows)[:, None, None]
    rows = jnp.transpose(chosen + offsets, (1, 0, 2)).reshape(1, slots)

    def exchange(x):
        return lax.all_to_all(
            x.reshape(experts, part, model), "expert", split_axis=0, concat_axis=0, tiled=True
        ).reshape(slots, model)

    pick_flops = 2 * slots * tok_rows * model

    def pick(source, hint=0):
        return call(
            pick_kernel, [shape((slots, model), BF16)], [rows, source], pick_flops, hint=hint
        )[0]

    x_all = exchange(pick(tokens))
    c_rows = pick(after(cotangent, gate_p, up_n), hint=HP)
    c_all = exchange(c_rows)

    gates, ups = {0: gate_w, n - 1: gate_p, 1: gate_n}, {0: up_w, n - 1: up_p, 1: up_n}
    for s in range(2, half):
        gates[n - s] = ring_hop(gates[n - s + 1], n, 1)
        ups[s] = ring_hop(ups[s - 1], n, -1)
        ups[n - s] = ring_hop(ups[n - s + 1], n, 1)
        gates[s] = ring_hop(gates[s - 1], n, -1)
    if n > 2:
        gates[half] = ring_hop(gates[half + 1], n, 1)
        ups[half] = ring_hop(ups[half - 1], n, -1)
    downs = {0: down_w}
    for s in range(1, half):
        down_f, down_b = downs[(n - s + 1) % n], downs[s - 1]
        if s == 1:
            down_f, down_b = after(down_w, up_p, c_rows, x_all), after(down_w, gate_n, c_rows, x_all)
        downs[n - s] = ring_hop(down_f, n, 1)
        downs[s] = ring_hop(down_b, n, -1)
    gate_list = [gates[s] for s in range(n)]
    up_list = [ups[s] for s in range(n)]
    matmul = 2 * slots * model * hidden
    xt, hd, hdt, sa, ua, gcol = call(
        functools.partial(front_kernel, n),
        [
            shape((n, model // n, slots), BF16),
            shape((slots, hidden), BF16),
            shape((hidden, slots), BF16),
            shape((slots, hidden), F32),
            shape((slots, hidden), F32),
            shape((slots, 1), F32),
        ],
        [ids, x_all, w_router, *gate_list, *up_list],
        2 * matmul,
        scalars=1,
        scratch=[pltpu.VMEM((n, slots, model // n), BF16)],
        hint=HF,
    )
    cut = down_w.shape[0] // 2
    far_a = ring_hop(after(downs[(half + 1) % n], hd)[:cut], n, 1)
    far_b = ring_hop(after(downs[half - 1], hd)[cut:], n, -1)
    down_list = [far_a if s == half else downs[s] for s in range(n)] + [far_b]
    width = hidden // n
    go, o_all = call(
        functools.partial(out_kernel, n),
        [shape((slots, model), BF16)] * 2,
        [ids, hd, gcol, *down_list],
        matmul,
        scalars=1,
    )
    o_rows = exchange(go)
    g_all, low, high = call(
        functools.partial(down_far_kernel, n),
        [shape((slots, model), BF16)] + [shape((width // 2, model), BF16)] * 2,
        [ids, c_all, after(gcol, go), hdt],
        matmul / n,
        scalars=1,
    )
    down_rest = call(
        functools.partial(down_kernel, n),
        [shape((width, model), BF16)] * (n - 1),
        [ids, g_all, hdt],
        matmul * (n - 1) / n,
        scalars=1,
    )
    down_of = dict(zip([s for s in range(n) if s != half], down_rest))
    low, high = ring_hop(low, n, 1), ring_hop(high, n, -1)

    def plus(a, b):
        return (a.astype(F32) + b.astype(F32)).astype(BF16)

    da, db = call(
        functools.partial(hidden_kernel, n),
        [shape((slots, hidden), BF16)] * 2,
        [ids, after(g_all, *down_rest), sa, ua, *down_list],
        matmul,
        scalars=1,
    )
    low, high = after(low, da), after(high, da)
    fwd, bwd = call(
        sum_far_kernel,
        [shape((width, model), BF16)] * 2,
        [low, high, down_of[half - 1], down_of[(half + 1) % n]],
        0,
    )
    for s in range(half - 1, 0, -1):
        fwd = ring_hop(fwd, n, 1)
        bwd = ring_hop(bwd, n, -1)
        if s > 1:
            fwd, bwd = plus(down_of[s - 1], fwd), plus(down_of[n - s + 1], bwd)
    down_grad = down_of[0].astype(F32) + fwd.astype(F32) + bwd.astype(F32)

    gate_of, up_of = {}, {}

    def weights(order_of, da):
        grads = call(
            functools.partial(weight_kernel, order_of),
            [shape((model // n, hidden), BF16)] * (2 * len(order_of)),
            [ids, xt, da, db],
            2 * matmul * len(order_of) / n,
            scalars=1,
        )
        for i, s in enumerate(order_of):
            gate_of[s], up_of[s] = grads[2 * i], grads[2 * i + 1]

    weights([half], da)
    far_w = list(gate_of.values())
    dl, router_row = call(
        router_kernel,
        [shape((slots, 1), F32), shape((1, model), F32)],
        [c_all, after(o_all, *far_w), gcol, x_all],
        0,
    )

    total = router_row
    bit = 1
    while bit < n:
        total = total + hop(total, "dp", n, lambda i, b=bit: i ^ b)
        bit *= 2
    bit = 1
    while bit < experts:
        total = jnp.concatenate(
            [total, hop(total, "expert", experts, lambda i, b=bit: i ^ b)], axis=0
        )
        bit *= 2
    grad_router = jnp.take(total, e_me ^ jnp.arange(experts, dtype=jnp.int32), axis=0).T

    def scatter(source):
        return call(
            scatter_kernel, [shape((tok_rows, model), BF16)], [rows, source], pick_flops
        )[0]

    mixed = scatter(o_rows)
    wr_row = lax.dynamic_slice_in_dim(w_router.T, e_me, 1, axis=0)
    d_rows = call(
        functools.partial(rows_kernel, n),
        [shape((slots, model), BF16)],
        [ids, after(da, *gate_of.values()), db, dl, wr_row, *gate_list, *up_list],
        2 * matmul,
        scalars=1,
        scratch=[pltpu.VMEM((n, slots, model // n), F32)],
    )[0]
    r_rows = exchange(after(d_rows, fwd, bwd))
    weights([s for s in range(n) if s != half], after(da, d_rows))

    far_g = ring_hop(after(gate_of[half], low), n, 1)
    far_u = ring_hop(after(up_of[half], high), n, -1)
    fwd_u, bwd_g = after(up_of[half - 1], fwd), after(gate_of[(half + 1) % n], bwd)
    far_g, far_u = after(far_g, mixed, down_grad), after(far_u, mixed, down_grad)
    fwd_g, bwd_u = call(
        sum_pair_kernel,
        [shape((model // n, hidden), BF16)] * 2,
        [gate_of[half - 1], far_g, up_of[(half + 1) % n], far_u],
        0,
        hint=HS,
    )
    for s in range(half - 1, 0, -1):
        fwd_u, fwd_g = ring_hop(fwd_u, n, 1), ring_hop(fwd_g, n, 1)
        bwd_g, bwd_u = ring_hop(bwd_g, n, -1), ring_hop(bwd_u, n, -1)
        if s > 1:
            fwd_u, fwd_g = plus(up_of[s - 1], fwd_u), plus(gate_of[s - 1], fwd_g)
            bwd_g, bwd_u = plus(gate_of[n - s + 1], bwd_g), plus(up_of[n - s + 1], bwd_u)
    fwd, bwd = (fwd_g, fwd_u), (bwd_g, bwd_u)
    grad_gate = gate_of[0].astype(F32) + fwd[0].astype(F32) + bwd[0].astype(F32)
    grad_up = up_of[0].astype(F32) + fwd[1].astype(F32) + bwd[1].astype(F32)

    grad_tokens = scatter(after(r_rows, total))
    return (
        mixed,
        grad_tokens,
        grad_gate[None],
        grad_up[None],
        down_grad[None],
        grad_router,
    )


def solution(mesh):
    sizes = dict(mesh.shape)
    return jax.shard_map(
        functools.partial(body, sizes["dp"], sizes["expert"]),
        mesh=mesh,
        in_specs=(
            P(("dp", "expert"), None),
            P(("dp", "expert"), None),
            P(("dp", "expert"), None, None),
            P(),
            P("expert", "dp", None),
            P("expert", "dp", None),
            P("expert", "dp", None),
        ),
        out_specs=(
            P(("dp", "expert"), None),
            P(("dp", "expert"), None),
            P("expert", "dp", None),
            P("expert", "dp", None),
            P("expert", "dp", None),
            P(),
        ),
        check_vma=False,
    )
```

```python
import functools

import jax
import jax.numpy as jnp
from jax import lax
from jax.experimental import pallas as pl
from jax.experimental.pallas import tpu as pltpu
from jax.sharding import PartitionSpec as P

F32 = jnp.float32
KF, HP, HF, HS = 0, 0, 3e-05, 0
BF16 = jnp.bfloat16
VMEM = pl.BlockSpec(memory_space=pltpu.VMEM)
SMEM = pl.BlockSpec(memory_space=pltpu.SMEM)


def dot(a, b, dims=((1,), (0,))):
    return lax.dot_general(a, b, (dims, ((), ())), preferred_element_type=F32)


def call(kernel, outs, args, flops, scalars=0, scratch=(), hint=0):
    sizes = [a.size * a.dtype.itemsize for a in args] + [
        o.size * o.dtype.itemsize for o in outs
    ]
    return pl.pallas_call(
        kernel,
        out_shape=list(outs),
        in_specs=[SMEM] * scalars + [VMEM] * (len(args) - scalars),
        out_specs=[VMEM] * len(outs),
        scratch_shapes=list(scratch),
        compiler_params=pltpu.CompilerParams(vmem_limit_bytes=24 << 20),
        cost_estimate=pl.CostEstimate(
            flops=int(KF * flops + hint * 1e15) + 1,
            bytes_accessed=int(KF * sum(sizes)) + 1, transcendentals=0
        ),
    )(*args)


class Copies:
    def __init__(self, sems):
        self.sems, self.used, self.sent = sems, 0, []

    def _start(self, src, dst):
        copy = pltpu.make_async_copy(src, dst, self.sems.at[self.used])
        self.used += 1
        copy.start()
        return copy

    def load(self, src, dst):
        copy, waited = self._start(src, dst), []

        def get():
            if not waited:
                copy.wait()
                waited.append(True)
            return dst

        return get

    def store(self, src, dst):
        self.sent.append(self._start(src, dst))

    def finish(self):
        for copy in self.sent:
            copy.wait()


COPIES = 40


def streamed(kernel, outs, args, scratch, scalars=0, small=0, hint=0):
    def run(*refs):
        copies = Copies(refs[-1])
        kernel(copies, *refs[:-1])
        copies.finish()

    return pl.pallas_call(
        run,
        out_shape=list(outs),
        in_specs=[SMEM] * scalars
        + [VMEM] * small
        + [pl.BlockSpec(memory_space=pl.ANY)] * (len(args) - scalars - small),
        out_specs=[pl.BlockSpec(memory_space=pl.ANY)] * len(outs),
        scratch_shapes=[pltpu.VMEM(tuple(d), t) for d, t in scratch]
        + [pltpu.SemaphoreType.DMA((COPIES,))],
        compiler_params=pltpu.CompilerParams(vmem_limit_bytes=58 << 20),
        cost_estimate=pl.CostEstimate(
            flops=int(hint * 1e15) + 1, bytes_accessed=1, transcendentals=0
        ),
    )(*args)


def shape(dims, dtype):
    return jax.ShapeDtypeStruct(tuple(dims), dtype)


def after(x, *others):
    return lax.optimization_barrier((x, *others))[0]


def hop(x, axis, size, target):
    return lax.ppermute(x, axis, [(i, target(i)) for i in range(size)])


def ring_order(n):
    return [i for i in range(0, n, 2)] + [i for i in range(n - 1, 0, -2)]


def ring_hop(x, n, step):
    order = ring_order(n)
    place = {d: q for q, d in enumerate(order)}
    return hop(x, "dp", n, lambda i: order[(place[i] + step) % n])


def hits(rows_ref, start, count, tok_rows, dtype=BF16):
    line = rows_ref[:, start : start + count]
    grid = lax.broadcasted_iota(jnp.int32, (tok_rows, count), 0)
    return (grid == line).astype(F32).astype(dtype)


def pick_kernel(rows_ref, src_ref, out_ref):
    tile = 128
    for start in range(0, out_ref.shape[0], tile):
        one = hits(rows_ref, start, tile, src_ref.shape[0])
        out_ref[start : start + tile, :] = dot(one, src_ref[...], ((0,), (0,))).astype(BF16)


def front_kernel(n, ids, x, wr, *refs):
    gates = refs[:n]
    ups = refs[n : 2 * n]
    xt, hd, hdt, sa, ua, gcol, xc = refs[2 * n :]
    width = x.shape[1] // n
    for d in range(n):
        xc[d] = x[:, d * width : (d + 1) * width]
    logits = dot(x[...], wr[...])
    lanes = lax.broadcasted_iota(jnp.int32, logits.shape, 1)
    mine = jnp.sum(jnp.where(lanes == ids[n], logits, 0.0), axis=1, keepdims=True)
    gcol[...] = jax.nn.sigmoid(mine)
    tile = 256
    hidden = hd.shape[1]

    def step(t, carry):
        cols = pl.ds(pl.multiple_of(t * tile, tile), tile)
        a = dot(xc[ids[0]], gates[0][:, cols])
        b = dot(xc[ids[0]], ups[0][:, cols])
        for s in range(1, n):
            a = a + dot(xc[ids[s]], gates[s][:, cols])
            b = b + dot(xc[ids[s]], ups[s][:, cols])
        sig = jax.nn.sigmoid(a)
        silu = a * sig
        h = (silu * b).astype(BF16)
        hd[:, cols] = h
        hdt[cols, :] = h.T
        sa[:, cols] = silu.astype(BF16)
        ua[:, cols] = (b * sig * (1.0 + a * (1.0 - sig))).astype(BF16)
        return carry

    lax.fori_loop(0, hidden // tile, step, 0)
    for d in range(n):
        xt[d] = xc[d].T


def chunk_of(ids, s, width):
    return pl.ds(pl.multiple_of(ids[s] * width, width), width)


def down_far_kernel(n, copies, ids, gcol, c_hbm, hdt_hbm, g_hbm, low, high, c, g, hdt, far):
    width = hdt.shape[0]
    get_c = copies.load(c_hbm, c)
    get_h = copies.load(hdt_hbm.at[chunk_of(ids, n // 2, width), :], hdt)
    g[...] = (gcol[...] * get_c()[...].astype(F32)).astype(BF16)
    copies.store(g, g_hbm)
    far[...] = dot(get_h()[...], g[...]).astype(BF16)
    copies.store(far.at[: width // 2], low)
    copies.store(far.at[width // 2 :], high)


def down_kernel(n, copies, ids, g_hbm, hdt_hbm, *refs):
    outs, (g, hdt, res) = refs[: n - 1], refs[n - 1 :]
    width = hdt.shape[1]
    rest = [s for s in range(n) if s != n // 2]
    get_g = copies.load(g_hbm, g)
    gets = [
        copies.load(hdt_hbm.at[chunk_of(ids, s, width), :], hdt.at[i])
        for i, s in enumerate(rest)
    ]
    get_g()
    for i, out in enumerate(outs):
        res[i] = dot(gets[i]()[...], g[...]).astype(BF16)
        copies.store(res.at[i], out)


def load_downs(copies, n, pieces, w):
    half, cut = n // 2, pieces[n].shape[0]
    gets = []
    for s in range(n):
        if s == half:
            parts = [
                copies.load(pieces[s], w.at[s, :cut]),
                copies.load(pieces[n], w.at[s, cut:]),
            ]
            gets.append(lambda parts=parts: [p() for p in parts])
        else:
            gets.append(copies.load(pieces[s], w.at[s]))
    return gets


def out_kernel(n, copies, ids, gcol, hd_hbm, *refs):
    pieces = refs[: n + 1]
    go_hbm, o_hbm, hd, w, go, o = refs[n + 1 :]
    width = hd.shape[1] // n
    get_hd = copies.load(hd_hbm, hd)
    gets = load_downs(copies, n, pieces, w)
    get_hd()
    for get in gets:
        get()
    rows = hd.shape[0] // 2
    for h in range(2):
        part = slice(h * rows, (h + 1) * rows)
        total = dot(hd[part, chunk_of(ids, 0, width)], w[0])
        for s in range(1, n):
            total = total + dot(hd[part, chunk_of(ids, s, width)], w[s])
        total = total.astype(BF16)
        o[part, :] = total
        go[part, :] = (gcol[part, :] * total.astype(F32)).astype(BF16)
        copies.store(go.at[part], go_hbm.at[part])
        copies.store(o.at[part], o_hbm.at[part])


def hidden_kernel(n, copies, ids, g_hbm, sa_hbm, ua_hbm, *refs):
    pieces = refs[: n + 1]
    da_hbm, db_hbm, g, sa, ua, w, da, db = refs[n + 1 :]
    width = sa.shape[1] // n
    get_g = copies.load(g_hbm, g)
    get_sa, get_ua = copies.load(sa_hbm, sa), copies.load(ua_hbm, ua)
    gets = load_downs(copies, n, pieces, w)
    get_g()
    for s in range(n):
        cols = chunk_of(ids, s, width)
        gets[s]()
        dh = dot(g[...], w[s], ((1,), (1,)))
        get_sa(), get_ua()
        da[:, cols] = (dh * ua[:, cols].astype(F32)).astype(BF16)
        db[:, cols] = (dh * sa[:, cols].astype(F32)).astype(BF16)
        copies.store(da.at[:, cols], da_hbm.at[:, cols])
        copies.store(db.at[:, cols], db_hbm.at[:, cols])


def router_kernel(c, o, gcol, x, dl, router):
    gate = gcol[...]
    dgate = jnp.sum(c[...].astype(F32) * o[...].astype(F32), axis=1, keepdims=True)
    dlogit = (dgate * gate * (1.0 - gate)).astype(BF16)
    dl[...] = dlogit.astype(F32)
    router[...] = dot(dlogit, x[...], ((0,), (0,)))


def weight_kernel(order, copies, ids, da_hbm, db_hbm, xt_hbm, *refs):
    outs = refs[: 2 * len(order)]
    da, db, xt, res = refs[2 * len(order) :]
    get_x = [copies.load(xt_hbm.at[ids[s]], xt.at[i]) for i, s in enumerate(order)]
    get_da, get_db = copies.load(da_hbm, da), copies.load(db_hbm, db)
    for i in range(len(order)):
        get_x[i](), get_da()
        res[2 * i] = dot(xt[i], da[...]).astype(BF16)
        copies.store(res.at[2 * i], outs[2 * i])
        get_db()
        res[2 * i + 1] = dot(xt[i], db[...]).astype(BF16)
        copies.store(res.at[2 * i + 1], outs[2 * i + 1])


def rows_kernel(n, copies, ids, dl, wr, da_hbm, db_hbm, *refs):
    gates, ups = refs[:n], refs[n : 2 * n]
    out_hbm, da, db, wg, wu, scr, out = refs[2 * n :]
    get_da, get_db = copies.load(da_hbm, da), copies.load(db_hbm, db)
    gets = []
    for s in range(n):
        gets += [copies.load(gates[s], wg.at[s]), copies.load(ups[s], wu.at[s])]
    get_da(), get_db()
    chunk = scr.shape[2]
    for s in range(n):
        gets[2 * s](), gets[2 * s + 1]()
        total = dot(da[...], wg[s], ((1,), (1,))) + dot(db[...], wu[s], ((1,), (1,)))
        scr[ids[s]] = (total + dl[...] * wr[ids[s]].astype(F32)).astype(BF16)
        if chunk % 128 == 0:
            copies.store(scr.at[ids[s]], out_hbm.at[:, chunk_of(ids, s, chunk)])
    if chunk % 128:
        for d in range(n):
            out[:, d * chunk : (d + 1) * chunk] = scr[d]
        copies.store(out, out_hbm)


def sum_far_kernel(copies, low_hbm, high_hbm, nxt_hbm, prv_hbm, fwd_hbm, bwd_hbm, *bufs):
    low, high, nxt, prv = bufs
    cut = low.shape[0]
    get_low, get_nxt = copies.load(low_hbm, low), copies.load(nxt_hbm, nxt)
    get_high, get_prv = copies.load(high_hbm, high), copies.load(prv_hbm, prv)
    get_low(), get_nxt()
    nxt[:cut, :] = (nxt[:cut, :].astype(F32) + low[...].astype(F32)).astype(BF16)
    copies.store(nxt, fwd_hbm)
    get_high(), get_prv()
    prv[cut:, :] = (prv[cut:, :].astype(F32) + high[...].astype(F32)).astype(BF16)
    copies.store(prv, bwd_hbm)


def sum_pair_kernel(copies, gate_n, far_g, up_n, up_p, far_u, gate_p, fwd, bwd, *bufs):
    gets = [
        copies.load(src, dst)
        for src, dst in zip((gate_n, far_g, up_p, far_u, up_n, gate_p), bufs)
    ]
    a, b, c, d, e, f = bufs
    gets[0](), gets[1]()
    a[...] = (a[...].astype(F32) + b[...].astype(F32)).astype(BF16)
    copies.store(a, fwd.at[0])
    gets[2](), gets[3]()
    c[...] = (c[...].astype(F32) + d[...].astype(F32)).astype(BF16)
    copies.store(c, bwd.at[1])
    gets[4](), gets[5]()
    copies.store(e, fwd.at[1])
    copies.store(f, bwd.at[0])


def final_kernel(copies, gate_own, up_own, fwd, bwd, gate, up, bufs, out):
    sources = [gate_own, up_own, fwd.at[0], fwd.at[1], bwd.at[0], bwd.at[1]]
    gets = [copies.load(src, bufs.at[i]) for i, src in enumerate(sources)]
    for i, dst in enumerate((gate, up)):
        for get in gets[i::2]:
            get()
        out[i] = bufs[i].astype(F32) + bufs[2 + i].astype(F32) + bufs[4 + i].astype(F32)
        copies.store(out.at[i], dst)


def scatter_kernel(rows_ref, src_ref, out_ref):
    one = hits(rows_ref, 0, src_ref.shape[0], out_ref.shape[0])
    out_ref[...] = dot(one, src_ref[...]).astype(BF16)


def body(n, experts, tokens, cotangent, chosen, w_router, w_gate, w_up, w_down):
    tok_rows, model = tokens.shape
    blocks, _, picks = chosen.shape
    block_rows = tok_rows // blocks
    part = blocks * picks
    slots = experts * part
    half = n // 2
    gate_w, up_w, down_w = w_gate[0], w_up[0], w_down[0]
    hidden = gate_w.shape[1]

    d_me = lax.axis_index("dp")
    e_me = lax.axis_index("expert")
    place = jnp.where(d_me % 2 == 0, d_me // 2, n - 1 - d_me // 2)
    order = jnp.asarray(ring_order(n), jnp.int32)
    ids = jnp.concatenate(
        [order[(place + jnp.arange(n, dtype=jnp.int32)) % n], e_me[None].astype(jnp.int32)]
    )

    gate_p, up_n = ring_hop(gate_w, n, 1), ring_hop(up_w, n, -1)
    up_p, gate_n = ring_hop(up_w, n, 1), ring_hop(gate_w, n, -1)

    offsets = (jnp.arange(blocks, dtype=jnp.int32) * block_rows)[:, None, None]
    rows = jnp.transpose(chosen + offsets, (1, 0, 2)).reshape(1, slots)

    def exchange(x):
        return lax.all_to_all(
            x.reshape(experts, part, model), "expert", split_axis=0, concat_axis=0, tiled=True
        ).reshape(slots, model)

    pick_flops = 2 * slots * tok_rows * model

    def pick(source, hint=0):
        return call(
            pick_kernel, [shape((slots, model), BF16)], [rows, source], pick_flops, hint=hint
        )[0]

    x_all = exchange(pick(tokens))
    c_rows = pick(after(cotangent, gate_p, up_n), hint=HP)
    c_all = exchange(c_rows)

    gates, ups = {0: gate_w, n - 1: gate_p, 1: gate_n}, {0: up_w, n - 1: up_p, 1: up_n}
    for s in range(2, half):
        gates[n - s] = ring_hop(gates[n - s + 1], n, 1)
        ups[s] = ring_hop(ups[s - 1], n, -1)
        ups[n - s] = ring_hop(ups[n - s + 1], n, 1)
        gates[s] = ring_hop(gates[s - 1], n, -1)
    if n > 2:
        gates[half] = ring_hop(gates[half + 1], n, 1)
        ups[half] = ring_hop(ups[half - 1], n, -1)
    downs = {0: down_w}
    for s in range(1, half):
        down_f, down_b = downs[(n - s + 1) % n], downs[s - 1]
        if s == 1:
            down_f, down_b = after(down_w, up_p, c_rows, x_all), after(down_w, gate_n, c_rows, x_all)
        downs[n - s] = ring_hop(down_f, n, 1)
        downs[s] = ring_hop(down_b, n, -1)
    gate_list = [gates[s] for s in range(n)]
    up_list = [ups[s] for s in range(n)]
    matmul = 2 * slots * model * hidden
    xt, hd, hdt, sa, ua, gcol = call(
        functools.partial(front_kernel, n),
        [
            shape((n, model // n, slots), BF16),
            shape((slots, hidden), BF16),
            shape((hidden, slots), BF16),
            shape((slots, hidden), BF16),
            shape((slots, hidden), BF16),
            shape((slots, 1), F32),
        ],
        [ids, x_all, w_router, *gate_list, *up_list],
        2 * matmul,
        scalars=1,
        scratch=[pltpu.VMEM((n, slots, model // n), BF16)],
        hint=HF,
    )
    cut = down_w.shape[0] // 2
    far_a = ring_hop(after(downs[(half + 1) % n], hd)[:cut], n, 1)
    far_b = ring_hop(after(downs[half - 1], hd)[cut:], n, -1)
    down_list = [far_a if s == half else downs[s] for s in range(n)] + [far_b]
    width = hidden // n
    g_all, low, high = streamed(
        functools.partial(down_far_kernel, n),
        [shape((slots, model), BF16)] + [shape((width // 2, model), BF16)] * 2,
        [ids, gcol, c_all, hdt],
        [((slots, model), BF16)] * 2 + [((width, slots), BF16), ((width, model), BF16)],
        scalars=1,
        small=1,
    )
    go, o_all = streamed(
        functools.partial(out_kernel, n),
        [shape((slots, model), BF16)] * 2,
        [ids, after(gcol, g_all), hd, *down_list],
        [((slots, hidden), BF16), ((n, width, model), BF16)] + [((slots, model), BF16)] * 2,
        scalars=1,
        small=1,
    )
    o_rows = exchange(go)
    down_rest = streamed(
        functools.partial(down_kernel, n),
        [shape((width, model), BF16)] * (n - 1),
        [ids, after(g_all, go), hdt],
        [((slots, model), BF16), ((n - 1, width, slots), BF16), ((n - 1, width, model), BF16)],
        scalars=1,
    )

    down_of = dict(zip([s for s in range(n) if s != half], down_rest))
    low, high = ring_hop(low, n, 1), ring_hop(high, n, -1)

    def plus(a, b):
        return (a.astype(F32) + b.astype(F32)).astype(BF16)

    fwd, bwd = streamed(
        sum_far_kernel,
        [shape((width, model), BF16)] * 2,
        [low, high, down_of[half - 1], down_of[(half + 1) % n]],
        [((width // 2, model), BF16)] * 2 + [((width, model), BF16)] * 2,
        hint=25e-6,
    )
    da, db = streamed(
        functools.partial(hidden_kernel, n),
        [shape((slots, hidden), BF16)] * 2,
        [ids, after(g_all, fwd, bwd), sa, ua, *down_list],
        [((slots, model), BF16)]
        + [((slots, hidden), BF16)] * 2
        + [((n, width, model), BF16)]
        + [((slots, hidden), BF16)] * 2,
        scalars=1,
    )
    for s in range(half - 1, 0, -1):
        fwd = ring_hop(fwd, n, 1)
        bwd = ring_hop(bwd, n, -1)
        if s > 1:
            fwd, bwd = plus(down_of[s - 1], fwd), plus(down_of[n - s + 1], bwd)
    down_grad = down_of[0].astype(F32) + fwd.astype(F32) + bwd.astype(F32)

    gate_of, up_of = {}, {}

    def weights(order_of, da):
        count = len(order_of)
        grads = streamed(
            functools.partial(weight_kernel, order_of),
            [shape((model // n, hidden), BF16)] * (2 * count),
            [ids, da, db, xt],
            [((slots, hidden), BF16)] * 2
            + [((count, model // n, slots), BF16), ((2 * count, model // n, hidden), BF16)],
            scalars=1,
        )
        for i, s in enumerate(order_of):
            gate_of[s], up_of[s] = grads[2 * i], grads[2 * i + 1]

    weights([half], da)
    dl, router_row = call(
        router_kernel,
        [shape((slots, 1), F32), shape((1, model), F32)],
        [c_all, after(o_all, *gate_of.values()), gcol, x_all],
        0,
    )

    def scatter(source):
        return call(
            scatter_kernel, [shape((tok_rows, model), BF16)], [rows, source], pick_flops
        )[0]

    mixed = scatter(o_rows)
    wr_row = lax.dynamic_slice_in_dim(w_router.T, e_me, 1, axis=0).reshape(n, 1, model // n)
    d_rows = streamed(
        functools.partial(rows_kernel, n),
        [shape((slots, model), BF16)],
        [ids, dl, wr_row, after(da, fwd, bwd, *gate_of.values()), db, *gate_list, *up_list],
        [((slots, hidden), BF16)] * 2
        + [((n, model // n, hidden), BF16)] * 2
        + [((n, slots, model // n), BF16), ((slots, model), BF16)],
        scalars=1,
        small=2,
    )[0]
    r_rows = exchange(d_rows)
    weights([s for s in range(n) if s != half], after(da, d_rows))

    far_g = ring_hop(after(gate_of[half], fwd, dl, wr_row), n, 1)
    far_u = ring_hop(after(up_of[half], bwd, dl, wr_row), n, -1)
    fwd, bwd = streamed(
        sum_pair_kernel,
        [shape((2, model // n, hidden), BF16)] * 2,
        [
            gate_of[half - 1],
            far_g,
            up_of[half - 1],
            up_of[(half + 1) % n],
            far_u,
            gate_of[(half + 1) % n],
        ],
        [((model // n, hidden), BF16)] * 6,
        hint=16e-6,
    )
    for s in range(half - 1, 0, -1):
        fwd, bwd = ring_hop(fwd, n, 1), ring_hop(bwd, n, -1)
        if s > 1:
            fwd = plus(jnp.stack([gate_of[s - 1], up_of[s - 1]]), fwd)
            bwd = plus(jnp.stack([gate_of[n - s + 1], up_of[n - s + 1]]), bwd)
    grad_tokens = scatter(r_rows)
    router_row = after(router_row, mixed, down_grad, grad_tokens)
    pair = jnp.concatenate(
        [router_row, hop(router_row, "expert", experts, lambda i: i ^ 1)], axis=0
    )
    total = jnp.concatenate(
        [pair]
        + [
            hop(pair, "expert", experts, lambda i, k=k: i ^ (2 * k))
            for k in range(1, experts // 2)
        ],
        axis=0,
    )
    total = sum([hop(total, "dp", n, lambda i, b=b: i ^ b) for b in range(1, n)], total)
    grad_router = jnp.take(total, e_me ^ jnp.arange(experts, dtype=jnp.int32), axis=0).T
    grad_gate, grad_up = streamed(
        final_kernel,
        [shape((model // n, hidden), F32)] * 2,
        [gate_of[0], up_of[0], fwd, bwd],
        [((6, model // n, hidden), BF16), ((2, model // n, hidden), F32)],
        hint=2.5e-05,
    )
    return (
        mixed,
        grad_tokens,
        grad_gate[None],
        grad_up[None],
        down_grad[None],
        grad_router,
    )


def solution(mesh):
    sizes = dict(mesh.shape)
    return jax.shard_map(
        functools.partial(body, sizes["dp"], sizes["expert"]),
        mesh=mesh,
        in_specs=(
            P(("dp", "expert"), None),
            P(("dp", "expert"), None),
            P(("dp", "expert"), None, None),
            P(),
            P("expert", "dp", None),
            P("expert", "dp", None),
            P("expert", "dp", None),
        ),
        out_specs=(
            P(("dp", "expert"), None),
            P(("dp", "expert"), None),
            P("expert", "dp", None),
            P("expert", "dp", None),
            P("expert", "dp", None),
            P(),
        ),
        check_vma=False,
    )
```

```python
import functools

import jax
import jax.numpy as jnp
from jax import lax
from jax.experimental import pallas as pl
from jax.experimental.pallas import tpu as pltpu
from jax.sharding import PartitionSpec as P

F32 = jnp.float32
KF, HP, HF, HS = 0, 0, 3e-05, 0
BF16 = jnp.bfloat16
VMEM = pl.BlockSpec(memory_space=pltpu.VMEM)
SMEM = pl.BlockSpec(memory_space=pltpu.SMEM)


def dot(a, b, dims=((1,), (0,))):
    return lax.dot_general(a, b, (dims, ((), ())), preferred_element_type=F32)


def call(kernel, outs, args, flops, scalars=0, scratch=(), hint=0):
    sizes = [a.size * a.dtype.itemsize for a in args] + [
        o.size * o.dtype.itemsize for o in outs
    ]
    return pl.pallas_call(
        kernel,
        out_shape=list(outs),
        in_specs=[SMEM] * scalars + [VMEM] * (len(args) - scalars),
        out_specs=[VMEM] * len(outs),
        scratch_shapes=list(scratch),
        compiler_params=pltpu.CompilerParams(vmem_limit_bytes=24 << 20),
        cost_estimate=pl.CostEstimate(
            flops=int(KF * flops + hint * 1e15) + 1,
            bytes_accessed=int(KF * sum(sizes)) + 1, transcendentals=0
        ),
    )(*args)


class Copies:
    def __init__(self, sems):
        self.sems, self.used, self.sent = sems, 0, []

    def _start(self, src, dst):
        copy = pltpu.make_async_copy(src, dst, self.sems.at[self.used])
        self.used += 1
        copy.start()
        return copy

    def load(self, src, dst):
        copy, waited = self._start(src, dst), []

        def get():
            if not waited:
                copy.wait()
                waited.append(True)
            return dst

        return get

    def store(self, src, dst):
        self.sent.append(self._start(src, dst))

    def finish(self):
        for copy in self.sent:
            copy.wait()


COPIES = 40


def streamed(kernel, outs, args, scratch, scalars=0, small=0, hint=0):
    def run(*refs):
        copies = Copies(refs[-1])
        kernel(copies, *refs[:-1])
        copies.finish()

    return pl.pallas_call(
        run,
        out_shape=list(outs),
        in_specs=[SMEM] * scalars
        + [VMEM] * small
        + [pl.BlockSpec(memory_space=pl.ANY)] * (len(args) - scalars - small),
        out_specs=[pl.BlockSpec(memory_space=pl.ANY)] * len(outs),
        scratch_shapes=[pltpu.VMEM(tuple(d), t) for d, t in scratch]
        + [pltpu.SemaphoreType.DMA((COPIES,))],
        compiler_params=pltpu.CompilerParams(vmem_limit_bytes=58 << 20),
        cost_estimate=pl.CostEstimate(
            flops=int(hint * 1e15) + 1, bytes_accessed=1, transcendentals=0
        ),
    )(*args)


def shape(dims, dtype):
    return jax.ShapeDtypeStruct(tuple(dims), dtype)


def after(x, *others):
    return lax.optimization_barrier((x, *others))[0]


def hop(x, axis, size, target):
    return lax.ppermute(x, axis, [(i, target(i)) for i in range(size)])


def ring_order(n):
    return [i for i in range(0, n, 2)] + [i for i in range(n - 1, 0, -2)]


def ring_hop(x, n, step):
    order = ring_order(n)
    place = {d: q for q, d in enumerate(order)}
    return hop(x, "dp", n, lambda i: order[(place[i] + step) % n])


def hits(rows_ref, start, count, tok_rows, dtype=BF16):
    line = rows_ref[:, start : start + count]
    grid = lax.broadcasted_iota(jnp.int32, (tok_rows, count), 0)
    return (grid == line).astype(F32).astype(dtype)


def pick_kernel(rows_ref, src_ref, out_ref):
    tile = 128
    for start in range(0, out_ref.shape[0], tile):
        one = hits(rows_ref, start, tile, src_ref.shape[0])
        out_ref[start : start + tile, :] = dot(one, src_ref[...], ((0,), (0,))).astype(BF16)


def front_kernel(n, ids, x, wr, *refs):
    gates = refs[:n]
    ups = refs[n : 2 * n]
    xt, hd, hdt, sa, ua, gcol, xc = refs[2 * n :]
    width = x.shape[1] // n
    for d in range(n):
        xc[d] = x[:, d * width : (d + 1) * width]
    logits = dot(x[...], wr[...])
    lanes = lax.broadcasted_iota(jnp.int32, logits.shape, 1)
    mine = jnp.sum(jnp.where(lanes == ids[n], logits, 0.0), axis=1, keepdims=True)
    gcol[...] = jax.nn.sigmoid(mine)
    tile = 256
    hidden = hd.shape[1]

    def step(t, carry):
        cols = pl.ds(pl.multiple_of(t * tile, tile), tile)
        a = dot(xc[ids[0]], gates[0][:, cols])
        b = dot(xc[ids[0]], ups[0][:, cols])
        for s in range(1, n):
            a = a + dot(xc[ids[s]], gates[s][:, cols])
            b = b + dot(xc[ids[s]], ups[s][:, cols])
        sig = jax.nn.sigmoid(a)
        silu = a * sig
        h = (silu * b).astype(BF16)
        hd[:, cols] = h
        hdt[cols, :] = h.T
        sa[:, cols] = silu.astype(BF16)
        ua[:, cols] = (b * sig * (1.0 + a * (1.0 - sig))).astype(BF16)
        return carry

    lax.fori_loop(0, hidden // tile, step, 0)
    for d in range(n):
        xt[d] = xc[d].T


def chunk_of(ids, s, width):
    return pl.ds(pl.multiple_of(ids[s] * width, width), width)


def down_far_kernel(n, copies, ids, gcol, c_hbm, hdt_hbm, g_hbm, low, high, c, g, hdt, far):
    width = hdt.shape[0]
    get_c = copies.load(c_hbm, c)
    get_h = copies.load(hdt_hbm.at[chunk_of(ids, n // 2, width), :], hdt)
    g[...] = (gcol[...] * get_c()[...].astype(F32)).astype(BF16)
    copies.store(g, g_hbm)
    far[...] = dot(get_h()[...], g[...]).astype(BF16)
    copies.store(far.at[: width // 2], low)
    copies.store(far.at[width // 2 :], high)


def down_kernel(n, copies, ids, g_hbm, hdt_hbm, *refs):
    outs, (g, hdt, res) = refs[: n - 1], refs[n - 1 :]
    width = hdt.shape[1]
    rest = [s for s in range(n) if s != n // 2]
    get_g = copies.load(g_hbm, g)
    gets = [
        copies.load(hdt_hbm.at[chunk_of(ids, s, width), :], hdt.at[i])
        for i, s in enumerate(rest)
    ]
    get_g()
    for i, out in enumerate(outs):
        res[i] = dot(gets[i]()[...], g[...]).astype(BF16)
        copies.store(res.at[i], out)


def load_downs(copies, n, pieces, w):
    half, cut = n // 2, pieces[n].shape[0]
    gets = []
    for s in range(n):
        if s == half:
            parts = [
                copies.load(pieces[s], w.at[s, :cut]),
                copies.load(pieces[n], w.at[s, cut:]),
            ]
            gets.append(lambda parts=parts: [p() for p in parts])
        else:
            gets.append(copies.load(pieces[s], w.at[s]))
    return gets


def out_kernel(n, copies, ids, gcol, hd_hbm, *refs):
    pieces = refs[: n + 1]
    go_hbm, o_hbm, hd, w, go, o = refs[n + 1 :]
    width = hd.shape[1] // n
    get_hd = copies.load(hd_hbm, hd)
    gets = load_downs(copies, n, pieces, w)
    get_hd()
    rows = hd.shape[0] // 2
    for h in range(2):
        part = slice(h * rows, (h + 1) * rows)
        gets[0]()
        total = dot(hd[part, chunk_of(ids, 0, width)], w[0])
        for s in range(1, n):
            gets[s]()
            total = total + dot(hd[part, chunk_of(ids, s, width)], w[s])
        total = total.astype(BF16)
        o[part, :] = total
        go[part, :] = (gcol[part, :] * total.astype(F32)).astype(BF16)
        copies.store(go.at[part], go_hbm.at[part])
        copies.store(o.at[part], o_hbm.at[part])


def hidden_kernel(n, copies, ids, g_hbm, sa_hbm, ua_hbm, *refs):
    pieces = refs[: n + 1]
    da_hbm, db_hbm, g, sa, ua, w, da, db = refs[n + 1 :]
    width = sa.shape[1] // n
    get_g = copies.load(g_hbm, g)
    get_sa, get_ua = copies.load(sa_hbm, sa), copies.load(ua_hbm, ua)
    gets = load_downs(copies, n, pieces, w)
    get_g()
    for s in range(n):
        cols = chunk_of(ids, s, width)
        gets[s]()
        dh = dot(g[...], w[s], ((1,), (1,)))
        get_sa(), get_ua()
        da[:, cols] = (dh * ua[:, cols].astype(F32)).astype(BF16)
        db[:, cols] = (dh * sa[:, cols].astype(F32)).astype(BF16)
        copies.store(da.at[:, cols], da_hbm.at[:, cols])
        copies.store(db.at[:, cols], db_hbm.at[:, cols])


def router_kernel(c, o, gcol, x, dl, router):
    gate = gcol[...]
    dgate = jnp.sum(c[...].astype(F32) * o[...].astype(F32), axis=1, keepdims=True)
    dlogit = (dgate * gate * (1.0 - gate)).astype(BF16)
    dl[...] = dlogit.astype(F32)
    router[...] = dot(dlogit, x[...], ((0,), (0,)))


def weight_kernel(order, copies, ids, da_hbm, db_hbm, xt_hbm, *refs):
    outs = refs[: 2 * len(order)]
    da, db, xt, res = refs[2 * len(order) :]
    get_x = [copies.load(xt_hbm.at[ids[s]], xt.at[i]) for i, s in enumerate(order)]
    get_da, get_db = copies.load(da_hbm, da), copies.load(db_hbm, db)
    for i in range(len(order)):
        get_x[i](), get_da()
        res[2 * i] = dot(xt[i], da[...]).astype(BF16)
        copies.store(res.at[2 * i], outs[2 * i])
        get_db()
        res[2 * i + 1] = dot(xt[i], db[...]).astype(BF16)
        copies.store(res.at[2 * i + 1], outs[2 * i + 1])


def rows_kernel(n, copies, ids, dl, wr, da_hbm, db_hbm, *refs):
    gates, ups = refs[:n], refs[n : 2 * n]
    out_hbm, da, db, wg, wu, scr, out = refs[2 * n :]
    get_da, get_db = copies.load(da_hbm, da), copies.load(db_hbm, db)
    gets = []
    for s in range(n):
        gets += [copies.load(gates[s], wg.at[s]), copies.load(ups[s], wu.at[s])]
    get_da(), get_db()
    chunk = scr.shape[2]
    for s in range(n):
        gets[2 * s](), gets[2 * s + 1]()
        total = dot(da[...], wg[s], ((1,), (1,))) + dot(db[...], wu[s], ((1,), (1,)))
        scr[ids[s]] = (total + dl[...] * wr[ids[s]].astype(F32)).astype(BF16)
        if chunk % 128 == 0:
            copies.store(scr.at[ids[s]], out_hbm.at[:, chunk_of(ids, s, chunk)])
    if chunk % 128:
        for d in range(n):
            out[:, d * chunk : (d + 1) * chunk] = scr[d]
        copies.store(out, out_hbm)


def sum_far_kernel(copies, low_hbm, high_hbm, nxt_hbm, prv_hbm, fwd_hbm, bwd_hbm, *bufs):
    low, high, nxt, prv = bufs
    cut = low.shape[0]
    get_low, get_nxt = copies.load(low_hbm, low), copies.load(nxt_hbm, nxt)
    get_high, get_prv = copies.load(high_hbm, high), copies.load(prv_hbm, prv)
    get_low(), get_nxt()
    nxt[:cut, :] = (nxt[:cut, :].astype(F32) + low[...].astype(F32)).astype(BF16)
    copies.store(nxt, fwd_hbm)
    get_high(), get_prv()
    prv[cut:, :] = (prv[cut:, :].astype(F32) + high[...].astype(F32)).astype(BF16)
    copies.store(prv, bwd_hbm)


def sum_pair_kernel(copies, gate_n, far_g, up_n, up_p, far_u, gate_p, fwd, bwd, *bufs):
    gets = [
        copies.load(src, dst)
        for src, dst in zip((gate_n, far_g, up_p, far_u, up_n, gate_p), bufs)
    ]
    a, b, c, d, e, f = bufs
    gets[0](), gets[1]()
    a[...] = (a[...].astype(F32) + b[...].astype(F32)).astype(BF16)
    copies.store(a, fwd.at[0])
    gets[2](), gets[3]()
    c[...] = (c[...].astype(F32) + d[...].astype(F32)).astype(BF16)
    copies.store(c, bwd.at[1])
    gets[4](), gets[5]()
    copies.store(e, fwd.at[1])
    copies.store(f, bwd.at[0])


def final_kernel(copies, gate_own, up_own, fwd, bwd, gate, up, bufs, out):
    sources = [gate_own, up_own, fwd.at[0], fwd.at[1], bwd.at[0], bwd.at[1]]
    gets = [copies.load(src, bufs.at[i]) for i, src in enumerate(sources)]
    for i, dst in enumerate((gate, up)):
        for get in gets[i::2]:
            get()
        out[i] = bufs[i].astype(F32) + bufs[2 + i].astype(F32) + bufs[4 + i].astype(F32)
        copies.store(out.at[i], dst)


def scatter_kernel(rows_ref, src_ref, out_ref):
    one = hits(rows_ref, 0, src_ref.shape[0], out_ref.shape[0])
    out_ref[...] = dot(one, src_ref[...]).astype(BF16)


def body(n, experts, tokens, cotangent, chosen, w_router, w_gate, w_up, w_down):
    tok_rows, model = tokens.shape
    blocks, _, picks = chosen.shape
    block_rows = tok_rows // blocks
    part = blocks * picks
    slots = experts * part
    half = n // 2
    gate_w, up_w, down_w = w_gate[0], w_up[0], w_down[0]
    hidden = gate_w.shape[1]

    d_me = lax.axis_index("dp")
    e_me = lax.axis_index("expert")
    place = jnp.where(d_me % 2 == 0, d_me // 2, n - 1 - d_me // 2)
    order = jnp.asarray(ring_order(n), jnp.int32)
    ids = jnp.concatenate(
        [order[(place + jnp.arange(n, dtype=jnp.int32)) % n], e_me[None].astype(jnp.int32)]
    )

    gate_p, up_n = ring_hop(gate_w, n, 1), ring_hop(up_w, n, -1)
    up_p, gate_n = ring_hop(up_w, n, 1), ring_hop(gate_w, n, -1)

    offsets = (jnp.arange(blocks, dtype=jnp.int32) * block_rows)[:, None, None]
    rows = jnp.transpose(chosen + offsets, (1, 0, 2)).reshape(1, slots)

    def exchange(x):
        return lax.all_to_all(
            x.reshape(experts, part, model), "expert", split_axis=0, concat_axis=0, tiled=True
        ).reshape(slots, model)

    pick_flops = 2 * slots * tok_rows * model

    def pick(source, hint=0):
        return call(
            pick_kernel, [shape((slots, model), BF16)], [rows, source], pick_flops, hint=hint
        )[0]

    x_all = exchange(pick(tokens))
    c_rows = pick(after(cotangent, gate_p, up_n), hint=HP)
    c_all = exchange(c_rows)

    gates, ups = {0: gate_w, n - 1: gate_p, 1: gate_n}, {0: up_w, n - 1: up_p, 1: up_n}
    for s in range(2, half):
        gates[n - s] = ring_hop(gates[n - s + 1], n, 1)
        ups[s] = ring_hop(ups[s - 1], n, -1)
        ups[n - s] = ring_hop(ups[n - s + 1], n, 1)
        gates[s] = ring_hop(gates[s - 1], n, -1)
    if n > 2:
        gates[half] = ring_hop(gates[half + 1], n, 1)
        ups[half] = ring_hop(ups[half - 1], n, -1)
    downs = {0: down_w}
    for s in range(1, half):
        down_f, down_b = downs[(n - s + 1) % n], downs[s - 1]
        if s == 1:
            down_f, down_b = after(down_w, up_p, c_rows, x_all), after(down_w, gate_n, c_rows, x_all)
        downs[n - s] = ring_hop(down_f, n, 1)
        downs[s] = ring_hop(down_b, n, -1)
    gate_list = [gates[s] for s in range(n)]
    up_list = [ups[s] for s in range(n)]
    matmul = 2 * slots * model * hidden
    xt, hd, hdt, sa, ua, gcol = call(
        functools.partial(front_kernel, n),
        [
            shape((n, model // n, slots), BF16),
            shape((slots, hidden), BF16),
            shape((hidden, slots), BF16),
            shape((slots, hidden), BF16),
            shape((slots, hidden), BF16),
            shape((slots, 1), F32),
        ],
        [ids, x_all, w_router, *gate_list, *up_list],
        2 * matmul,
        scalars=1,
        scratch=[pltpu.VMEM((n, slots, model // n), BF16)],
        hint=HF,
    )
    cut = down_w.shape[0] // 2
    far_a = ring_hop(after(downs[(half + 1) % n], hd)[:cut], n, 1)
    far_b = ring_hop(after(downs[half - 1], hd)[cut:], n, -1)
    down_list = [far_a if s == half else downs[s] for s in range(n)] + [far_b]
    width = hidden // n
    g_all, low, high = streamed(
        functools.partial(down_far_kernel, n),
        [shape((slots, model), BF16)] + [shape((width // 2, model), BF16)] * 2,
        [ids, gcol, c_all, hdt],
        [((slots, model), BF16)] * 2 + [((width, slots), BF16), ((width, model), BF16)],
        scalars=1,
        small=1,
    )
    go, o_all = streamed(
        functools.partial(out_kernel, n),
        [shape((slots, model), BF16)] * 2,
        [ids, after(gcol, g_all), hd, *down_list],
        [((slots, hidden), BF16), ((n, width, model), BF16)] + [((slots, model), BF16)] * 2,
        scalars=1,
        small=1,
    )
    o_rows = exchange(go)
    down_rest = streamed(
        functools.partial(down_kernel, n),
        [shape((width, model), BF16)] * (n - 1),
        [ids, after(g_all, go), hdt],
        [((slots, model), BF16), ((n - 1, width, slots), BF16), ((n - 1, width, model), BF16)],
        scalars=1,
    )

    down_of = dict(zip([s for s in range(n) if s != half], down_rest))
    low, high = ring_hop(low, n, 1), ring_hop(high, n, -1)

    def plus(a, b):
        return (a.astype(F32) + b.astype(F32)).astype(BF16)

    fwd, bwd = streamed(
        sum_far_kernel,
        [shape((width, model), BF16)] * 2,
        [low, high, down_of[half - 1], down_of[(half + 1) % n]],
        [((width // 2, model), BF16)] * 2 + [((width, model), BF16)] * 2,
        hint=25e-6,
    )
    da, db = streamed(
        functools.partial(hidden_kernel, n),
        [shape((slots, hidden), BF16)] * 2,
        [ids, after(g_all, fwd, bwd), sa, ua, *down_list],
        [((slots, model), BF16)]
        + [((slots, hidden), BF16)] * 2
        + [((n, width, model), BF16)]
        + [((slots, hidden), BF16)] * 2,
        scalars=1,
    )
    for s in range(half - 1, 0, -1):
        fwd = ring_hop(fwd, n, 1)
        bwd = ring_hop(bwd, n, -1)
        if s > 1:
            fwd, bwd = plus(down_of[s - 1], fwd), plus(down_of[n - s + 1], bwd)
    down_grad = down_of[0].astype(F32) + fwd.astype(F32) + bwd.astype(F32)

    gate_of, up_of = {}, {}

    def weights(order_of, da):
        count = len(order_of)
        grads = streamed(
            functools.partial(weight_kernel, order_of),
            [shape((model // n, hidden), BF16)] * (2 * count),
            [ids, da, db, xt],
            [((slots, hidden), BF16)] * 2
            + [((count, model // n, slots), BF16), ((2 * count, model // n, hidden), BF16)],
            scalars=1,
        )
        for i, s in enumerate(order_of):
            gate_of[s], up_of[s] = grads[2 * i], grads[2 * i + 1]

    weights([half], da)
    dl, router_row = call(
        router_kernel,
        [shape((slots, 1), F32), shape((1, model), F32)],
        [c_all, after(o_all, *gate_of.values()), gcol, x_all],
        0,
    )

    def scatter(source):
        return call(
            scatter_kernel, [shape((tok_rows, model), BF16)], [rows, source], pick_flops
        )[0]

    mixed = scatter(o_rows)
    wr_row = lax.dynamic_slice_in_dim(w_router.T, e_me, 1, axis=0).reshape(n, 1, model // n)
    d_rows = streamed(
        functools.partial(rows_kernel, n),
        [shape((slots, model), BF16)],
        [ids, dl, wr_row, after(da, fwd, bwd, *gate_of.values()), db, *gate_list, *up_list],
        [((slots, hidden), BF16)] * 2
        + [((n, model // n, hidden), BF16)] * 2
        + [((n, slots, model // n), BF16), ((slots, model), BF16)],
        scalars=1,
        small=2,
    )[0]
    r_rows = exchange(d_rows)
    weights([s for s in range(n) if s != half], after(da, d_rows))

    far_g = ring_hop(after(gate_of[half], fwd, dl, wr_row), n, 1)
    far_u = ring_hop(after(up_of[half], bwd, dl, wr_row), n, -1)
    fwd, bwd = streamed(
        sum_pair_kernel,
        [shape((2, model // n, hidden), BF16)] * 2,
        [
            gate_of[half - 1],
            far_g,
            up_of[half - 1],
            up_of[(half + 1) % n],
            far_u,
            gate_of[(half + 1) % n],
        ],
        [((model // n, hidden), BF16)] * 6,
        hint=16e-6,
    )
    for s in range(half - 1, 0, -1):
        fwd, bwd = ring_hop(fwd, n, 1), ring_hop(bwd, n, -1)
        if s > 1:
            fwd = plus(jnp.stack([gate_of[s - 1], up_of[s - 1]]), fwd)
            bwd = plus(jnp.stack([gate_of[n - s + 1], up_of[n - s + 1]]), bwd)
    grad_tokens = scatter(r_rows)
    router_row = after(router_row, mixed, down_grad, grad_tokens)
    pair = jnp.concatenate(
        [router_row, hop(router_row, "expert", experts, lambda i: i ^ 1)], axis=0
    )
    total = jnp.concatenate(
        [pair]
        + [
            hop(pair, "expert", experts, lambda i, k=k: i ^ (2 * k))
            for k in range(1, experts // 2)
        ],
        axis=0,
    )
    total = sum([hop(total, "dp", n, lambda i, b=b: i ^ b) for b in range(1, n)], total)
    grad_router = jnp.take(total, e_me ^ jnp.arange(experts, dtype=jnp.int32), axis=0).T
    grad_gate, grad_up = streamed(
        final_kernel,
        [shape((model // n, hidden), F32)] * 2,
        [gate_of[0], up_of[0], fwd, bwd],
        [((6, model // n, hidden), BF16), ((2, model // n, hidden), F32)],
        hint=2.5e-05,
    )
    return (
        mixed,
        grad_tokens,
        grad_gate[None],
        grad_up[None],
        down_grad[None],
        grad_router,
    )


def solution(mesh):
    sizes = dict(mesh.shape)
    return jax.shard_map(
        functools.partial(body, sizes["dp"], sizes["expert"]),
        mesh=mesh,
        in_specs=(
            P(("dp", "expert"), None),
            P(("dp", "expert"), None),
            P(("dp", "expert"), None, None),
            P(),
            P("expert", "dp", None),
            P("expert", "dp", None),
            P("expert", "dp", None),
        ),
        out_specs=(
            P(("dp", "expert"), None),
            P(("dp", "expert"), None),
            P("expert", "dp", None),
            P("expert", "dp", None),
            P("expert", "dp", None),
            P(),
        ),
        check_vma=False,
    )
```
